32 devices in a mesh: ctx: 8 (over y, x, core), tp: 4 (over z).
Axes of the slice: x: 2, y: 2, z: 4, core: 2. Of those that a mesh axis runs over, the one named last changes fastest.
Arguments:
- gate: bfloat16 [3072, 8192], P('ctx', 'tp'), may hold values from -6 to 6
- key: bfloat16 [3072, 8192], P('ctx', 'tp'), may hold values from -6 to 6
- value: bfloat16 [3072, 8192], P('ctx', 'tp'), may hold values from -6 to 6
- filters: bfloat16 [128, 512], P(None, 'tp'), may hold values from -0.5 to 0.5
- lengths: int32 [16], replicated, may hold values from 1 to 1536, 3072 in all
- cotangent: bfloat16 [3072, 8192], P('ctx', 'tp'), may hold values from -6 to 6
Outputs:
- gate_grad: bfloat16 [3072, 8192], P('ctx', 'tp')
- key_grad: bfloat16 [3072, 8192], P('ctx', 'tp')
- value_grad: bfloat16 [3072, 8192], P('ctx', 'tp')
- filter_grad: float32 [128, 512], P('ctx', 'tp')
The draws below stay inside these ranges and needn't reach their ends.
All inputs are finite; a program needn't handle non-finite values.
Results may differ from the reference program's by a relative error of at most 0.0049.
Values may be sent and summed in bfloat16 or wider, within the bound.
A program may use at most 128 MiB of HBM per device.

```python
import math
import jax
import jax.numpy as jnp
import numpy as np
from jax import lax

D = 8192
TAPS = 128
CPG = 16
TOKENS = 3072
NDOCS = 16
MOST = 1536
FG = 512


def steps_of(rng, extent, pieces, low, high):
    def one(position, shards_of):
        steps = jax.random.uniform(jax.random.fold_in(jax.random.fold_in(rng, 6), position), (shards_of,), jnp.float32, low / len(pieces), high / len(pieces))
        return jnp.repeat(jnp.exp(steps), extent[position] // shards_of).reshape((-1,) + (1,) * (len(extent) - position - 1))

    gain = one(*pieces[0])
    for cut in pieces[1:]:
        gain = gain * one(*cut)
    return gain


def length_profile(number_of, total, reach, slope):
    weights = [(1 << 20) // math.isqrt(rank ** slope) + 1 for rank in range(2, number_of + 1)]
    surplus, given = total - reach - (number_of - 1), [1] * (number_of - 1)
    while surplus > 0:
        movable = [i for i in range(number_of - 1) if given[i] < reach]
        mass, remaining = sum([weights[i] for i in movable]), surplus
        for i in movable:
            more = min(reach - given[i], max(1, remaining * weights[i] // mass), surplus)
            given[i] = given[i] + more
            surplus = surplus - more
    return np.array([reach] + given)


def ragged(stream_key, count, total, most, skew):
    if count == 2:
        one = jax.random.randint(stream_key, (), max(1, total - most), min(most, total - 1) + 1)
        return jnp.stack([one, total - one])
    tallies = jnp.asarray(length_profile(count, total, most, skew), jnp.int32)
    pairs = (count - 1) // 2
    giver, sink = tallies[1:1 + 2 * pairs:2], tallies[2:2 + 2 * pairs:2]
    slack = jnp.minimum(giver - 1, most - sink)
    passed = jax.random.randint(jax.random.fold_in(stream_key, 1), (pairs,), 0, 1 << 20) % (slack + 1)
    tallies = tallies.at[1:1 + 2 * pairs:2].set(giver - passed).at[2:2 + 2 * pairs:2].set(sink + passed)
    return tallies[jax.random.permutation(jax.random.fold_in(stream_key, 2), count)]


def bell_draw(key, dims, width, reach, split=(), kind=jnp.bfloat16):
    level = steps_of(key, dims, split, -0.22, 0.18) if split else 1.0
    values = jax.random.normal(key, dims, jnp.float32) * width * level
    return jnp.minimum(jnp.maximum(values, -reach), reach).astype(kind)


def setup_inputs(seed: int = 0) -> dict:
    keys = jax.random.split(jax.random.key(seed), 7)
    return {
        "gate": bell_draw(keys[0], (TOKENS, D), 1.0, 6.0, ((0, 8), (1, 4))),
        "key": bell_draw(keys[1], (TOKENS, D), 1.0, 6.0, ((0, 8), (1, 4))),
        "value": bell_draw(keys[2], (TOKENS, D), 1.0, 6.0, ((0, 8), (1, 4))),
        "filters": bell_draw(keys[3], (TAPS, FG), TAPS ** -0.5, 0.5, ((1, 4),)),
        "lengths": ragged(keys[4], NDOCS, TOKENS, MOST, 2).astype(jnp.int32),
        "cotangent": bell_draw(keys[5], (TOKENS, D), 1.0, 6.0, ((0, 8), (1, 4))),
    }


def band_table(tap_cols):
    tap_count, group_count = tap_cols.shape
    flipped = jnp.flip(tap_cols.T, axis=1)
    padded = jnp.concatenate([jnp.zeros((group_count, 1), tap_cols.dtype), flipped, jnp.zeros((group_count, tap_count), tap_cols.dtype)], axis=1)
    tiled_rows = jnp.broadcast_to(padded[:, None, :], (group_count, tap_count, 2 * tap_count + 1))
    flat_rows = tiled_rows.reshape(group_count, tap_count * (2 * tap_count + 1))
    return flat_rows[:, :2 * tap_count * tap_count].reshape(group_count, tap_count, 2 * tap_count)

def block_mask(lengths, first_row, tap_count):
    doc_ends = jnp.cumsum(lengths).astype(jnp.int32)
    row_ids = (first_row + jnp.arange(tap_count, dtype=jnp.int32)).astype(jnp.int32)
    doc_starts = lax.optimization_barrier(jnp.sum(jnp.where(doc_ends[None, :] <= row_ids[:, None], lengths[None, :], 0), axis=1)).astype(jnp.int32)
    col_ids = (first_row - tap_count + jnp.arange(2 * tap_count, dtype=jnp.int32)).astype(jnp.int32)
    return col_ids[None, :] >= doc_starts[:, None]

def reference(gate, key, value, filters, lengths, cotangent):
    highest = lax.Precision.HIGHEST
    per_group = 8
    group_count = FG // per_group
    group_width = per_group * CPG
    block_count = TOKENS // TAPS
    firsts = jnp.arange(block_count, dtype=jnp.int32) * TAPS
    doc_masks = jax.vmap(lambda first_row: block_mask(lengths, first_row, TAPS))(firsts)
    grad_scale = 1.0 / math.sqrt(TOKENS)

    def split_groups(array):
        return array.reshape(TOKENS, group_count, group_width).transpose(1, 0, 2)
    filt_groups = filters.reshape(TAPS, group_count, per_group).transpose(1, 0, 2)

    def one_group(operands):
        gate_g, key_g, value_g, cot_g, filt_g = operands
        key_float = key_g.astype(jnp.float32)
        value_float = value_g.astype(jnp.float32)
        product = (key_float * value_float).astype(jnp.bfloat16)
        filt_float = filt_g.astype(jnp.float32)
        band_tab = band_table(filt_float)
        banded = jnp.where(doc_masks[:, None], band_tab[None], 0.0)
        extended = jnp.concatenate([jnp.zeros((TAPS, group_width), jnp.bfloat16), product], axis=0)
        windows = jnp.concatenate([extended[:TOKENS].reshape(block_count, TAPS, group_width), extended[TAPS:].reshape(block_count, TAPS, group_width)], axis=1)
        windows = windows.reshape(block_count, 2 * TAPS, per_group, CPG).astype(jnp.float32)
        filtered = jnp.einsum('nfab,nbfc->nafc', banded, windows, precision=highest).reshape(TOKENS, group_width)
        cot_float = cot_g.astype(jnp.float32)
        filt_cot = (cot_float * gate_g.astype(jnp.float32)).astype(jnp.bfloat16)
        gate_grad = (cot_float * filtered).astype(jnp.bfloat16)
        cot_blocks = filt_cot.astype(jnp.float32).reshape(block_count, TAPS, per_group, CPG)
        spread = jnp.einsum('nfab,nafc->nbfc', banded, cot_blocks, precision=highest)
        later_part = jnp.concatenate([spread[1:, :TAPS], jnp.zeros((1, TAPS, per_group, CPG), jnp.float32)], axis=0)
        prod_grad = (spread[:, TAPS:] + later_part).reshape(TOKENS, group_width)
        key_grad = (prod_grad * value_float).astype(jnp.bfloat16)
        value_grad = (prod_grad * key_float).astype(jnp.bfloat16)
        correl = jnp.einsum('nafc,nbfc->nfab', cot_blocks, windows, precision=highest)
        corr_sum = lax.optimization_barrier(jnp.sum(jnp.where(doc_masks[:, None], correl, 0.0), axis=0))
        filter_grad = jax.vjp(band_table, filt_float)[1](corr_sum)[0] * grad_scale
        return (gate_grad, key_grad, value_grad, filter_grad)
    results = lax.map(one_group, (split_groups(gate), split_groups(key), split_groups(value), split_groups(cotangent), filt_groups))
    gate_grad = results[0].transpose(1, 0, 2).reshape(TOKENS, D)
    key_grad = results[1].transpose(1, 0, 2).reshape(TOKENS, D)
    value_grad = results[2].transpose(1, 0, 2).reshape(TOKENS, D)
    filter_grad = results[3].transpose(1, 0, 2).reshape(TAPS, FG)
    return (gate_grad, key_grad, value_grad, filter_grad)
```

```python
import functools
import math

import jax
import jax.numpy as jnp
from jax import lax
from jax.experimental import pallas as pl
from jax.experimental.pallas import tpu as pltpu
from jax.sharding import PartitionSpec as P

BF = jnp.bfloat16
F32 = jnp.float32
CHUNK = 128


def passed_along(value, axis, steps):
    count = lax.axis_size(axis)
    first, last = (max(0, -steps), min(count, count - steps))
    return lax.ppermute(value, axis, [(source, source + steps) for source in range(first, last)])


def doc_ids(lengths_ref, first, shape, dim):
    tokens = first + lax.broadcasted_iota(jnp.int32, shape, dim)

    def add(d, carry):
        end, ids = carry
        end = end + lengths_ref[d]
        return (end, ids + jnp.where(tokens >= end, 1, 0))

    return lax.fori_loop(
        0, lengths_ref.shape[0], add, (jnp.int32(0), jnp.zeros(shape, jnp.int32)), unroll=4
    )[1]


def fill_masks(lengths_ref, row_base, fwd, bwd, mask_f, mask_b, mask_c):
    taps = CHUNK
    row = lax.broadcasted_iota(jnp.int32, (taps, taps), 0)
    col = lax.broadcasted_iota(jnp.int32, (taps, taps), 1)
    for i, n in enumerate(fwd):
        first = row_base + n * taps
        mine = doc_ids(lengths_ref, first, (taps, taps), 0)
        prev = doc_ids(lengths_ref, first - taps, (8, taps), 1)[:1]
        cur = doc_ids(lengths_ref, first, (8, taps), 1)[:1]
        left = jnp.where((mine == prev) & (col > row), 1.0, 0.0)
        right = jnp.where((mine == cur) & (col <= row), 1.0, 0.0)
        mask_f[i, :, :taps] = left.astype(BF)
        mask_f[i, :, taps:] = right.astype(BF)
        mask_c[i, :, :taps] = left
        mask_c[i, :, taps:] = right
    for i, n in enumerate(bwd):
        first = row_base + n * taps
        mine = doc_ids(lengths_ref, first, (taps, taps), 0)
        cur = doc_ids(lengths_ref, first, (8, taps), 1)[:1]
        later = doc_ids(lengths_ref, first + taps, (8, taps), 1)[:1]
        left = jnp.where((mine == cur) & (col >= row), 1.0, 0.0)
        right = jnp.where((mine == later) & (col < row), 1.0, 0.0)
        mask_b[i, :, :taps] = left.astype(BF)
        mask_b[i, :, taps:] = right.astype(BF)


def fill_taps(filters_ref, taps_f, taps_b):
    taps, count = filters_ref.shape
    row = lax.broadcasted_iota(jnp.int32, (taps, taps), 0)
    col = lax.broadcasted_iota(jnp.int32, (taps, taps), 1)
    same = jnp.where(row == col, 1.0, 0.0).astype(BF)
    flip = jnp.where(((row + col) & (taps - 1)) == 0, 1.0, 0.0).astype(BF)
    dims = (((0,), (0,)), ((), ()))
    table = filters_ref[...]
    taps_b[...] = lax.dot_general(table, same, dims, preferred_element_type=F32)
    taps_f[...] = lax.dot_general(table, flip, dims, preferred_element_type=F32)


def convolve(tap_rows, masks, inputs, chan_group):
    taps = CHUNK
    lane = lax.broadcasted_iota(jnp.int32, (taps, taps), 1)
    per = tap_rows.shape[0]
    totals = [None] * len(inputs)
    for f in range(per):
        spread = jnp.broadcast_to(tap_rows[f : f + 1], (taps, taps))
        circ = pltpu.roll(spread, 0, 1, stride=1, stride_axis=0).astype(BF)
        both = jnp.concatenate([circ, circ], axis=1)
        mine = lane >= f * chan_group
        for i, x in enumerate(inputs):
            got = jnp.dot(both * masks[i], x, preferred_element_type=F32)
            totals[i] = got if f == 0 else jnp.where(mine, got, totals[i])
    return totals


def correlate(cots, windows, masks, per, chan_group):
    taps = CHUNK
    lane = lax.broadcasted_iota(jnp.int32, (1, taps), 1)
    sums = []
    for f in range(per):
        mine = jnp.where(
            (lane >= f * chan_group) & (lane < (f + 1) * chan_group), 1.0, 0.0
        ).astype(BF)
        total = None
        for cot, window, mask in zip(cots, windows, masks):
            got = lax.dot_general(
                cot * mine, window, (((1,), (1,)), ((), ())), preferred_element_type=F32
            )
            got = got * mask[...]
            got = got[:, :taps] + got[:, taps:]
            total = got if total is None else total + got
        held = total[:8]
        for q in range(1, taps // 8):
            held = held + pltpu.roll(total[8 * q : 8 * q + 8], taps - 8 * q, 1)
        sums.append(held)
    return sums


def collapse(corr_ref, scale):
    taps = CHUNK
    total = corr_ref[:, 0, :]
    for r in range(1, 8):
        total = total + pltpu.roll(corr_ref[:, r, :], taps - r, 1)
    row = lax.broadcasted_iota(jnp.int32, (taps, taps), 0)
    col = lax.broadcasted_iota(jnp.int32, (taps, taps), 1)
    flip = jnp.where(((row + col) & (taps - 1)) == 0, scale, 0.0)
    return lax.dot_general(
        flip, total, (((1,), (1,)), ((), ())),
        precision=lax.Precision.HIGHEST, preferred_element_type=F32,
    )


def inner_kernel(
    blocks, chan_group, base_ref, lengths_ref, filters_ref, gate_ref, key_ref, value_ref, cot_ref,
    gg_ref, kg_ref, vg_ref, corr_ref, taps_f, taps_b, mask_f, mask_b, mask_c,
):
    taps = CHUNK
    fwd, bwd = range(1, blocks), range(0, blocks - 1)

    @pl.when(pl.program_id(0) == 0)
    def _():
        fill_taps(filters_ref, taps_f, taps_b)
        fill_masks(lengths_ref, base_ref[0], fwd, bwd, mask_f, mask_b, mask_c)

    per = CHUNK // chan_group
    here = pl.ds(pl.multiple_of(pl.program_id(0) * per, per), per)
    key = key_ref[...].astype(F32)
    value = value_ref[...].astype(F32)
    cot = cot_ref[...].astype(F32)
    product = (key * value).astype(BF)
    filt_cot = (cot * gate_ref[...].astype(F32)).astype(BF)
    windows = [product[(n - 1) * taps : (n + 1) * taps] for n in fwd]
    outs = convolve(taps_f[here], [mask_f.at[i][...] for i in range(len(fwd))], windows, chan_group)
    for n, out in zip(fwd, outs):
        rows = slice(n * taps, (n + 1) * taps)
        gg_ref[rows] = (cot[rows] * out).astype(BF)
    ahead = [filt_cot[n * taps : (n + 2) * taps] for n in bwd]
    outs = convolve(taps_b[here], [mask_b.at[i][...] for i in range(len(bwd))], ahead, chan_group)
    for n, out in zip(bwd, outs):
        rows = slice(n * taps, (n + 1) * taps)
        kg_ref[rows] = (out * value[rows]).astype(BF)
        vg_ref[rows] = (out * key[rows]).astype(BF)
    cots = [filt_cot[n * taps : (n + 1) * taps] for n in fwd]
    sums = correlate(cots, windows, [mask_c.at[i] for i in range(len(fwd))], per, chan_group)
    for f in range(per):
        corr_ref[pl.program_id(0) * per + f] = sums[f]


def edge_kernel(
    blocks, chan_group, scale, base_ref, lengths_ref, filters_ref, prev_ref, next_ref,
    key_ref, value_ref, key_last, value_last, gate_ref, cot_ref, gate_last, cot_last,
    part_ref, gg_in, kg_in, vg_in,
    gg_ref, kg_ref, vg_ref, grad_ref, taps_f, taps_b, mask_f, mask_b, mask_c, corr_ref,
):
    taps = CHUNK
    steps = pl.num_programs(0)

    @pl.when(pl.program_id(0) == 0)
    def _():
        fill_taps(filters_ref, taps_f, taps_b)
        fill_masks(lengths_ref, base_ref[0], [0], [blocks - 1], mask_f, mask_b, mask_c)

    per = CHUNK // chan_group
    here = pl.ds(pl.multiple_of(pl.program_id(0) * per, per), per)
    cot = cot_ref[...].astype(F32)
    product = (key_ref[...].astype(F32) * value_ref[...].astype(F32)).astype(BF)
    filt_cot = (cot * gate_ref[...].astype(F32)).astype(BF)
    window = jnp.concatenate([prev_ref[...], product], axis=0)
    out = convolve(taps_f[here], [mask_f[0]], [window], chan_group)[0]
    gg_ref[...] = (cot * out).astype(BF)
    last_cot = (cot_last[...].astype(F32) * gate_last[...].astype(F32)).astype(BF)
    ahead = jnp.concatenate([last_cot, next_ref[...]], axis=0)
    out = convolve(taps_b[here], [mask_b[0]], [ahead], chan_group)[0]
    kg_ref[...] = (out * value_last[...].astype(F32)).astype(BF)
    vg_ref[...] = (out * key_last[...].astype(F32)).astype(BF)
    sums = correlate([filt_cot], [window], [mask_c.at[0]], per, chan_group)
    for f in range(per):
        at = pl.program_id(0) * per + f
        corr_ref[at] = part_ref[at] + sums[f]

    @pl.when(pl.program_id(0) == steps - 1)
    def _():
        grad_ref[...] = collapse(corr_ref, scale)


def on_device(gate, key, value, filters, lengths, cotangent):
    row_count, width = gate.shape
    taps, filt_count = filters.shape
    chan_group = width // filt_count
    blocks = row_count // taps
    ctx_count = lax.axis_size("ctx")
    base = (lax.axis_index("ctx") * row_count).astype(jnp.int32).reshape(1)
    scale = 1.0 / math.sqrt(row_count * ctx_count)
    tail = slice(row_count - taps, row_count)
    prev = passed_along(
        (key[tail].astype(F32) * value[tail].astype(F32)).astype(BF), "ctx", 1
    )
    later = passed_along(
        (cotangent[:taps].astype(F32) * gate[:taps].astype(F32)).astype(BF), "ctx", -1
    )
    steps = width // CHUNK
    smem = pl.BlockSpec(memory_space=pltpu.SMEM)
    whole = pl.BlockSpec((taps, filt_count), lambda g: (0, 0))
    strip = pl.BlockSpec((row_count, CHUNK), lambda g: (0, g))
    top = pl.BlockSpec((taps, CHUNK), lambda g: (0, g))
    bottom = pl.BlockSpec((taps, CHUNK), lambda g: (blocks - 1, g))
    table = pl.BlockSpec((filt_count, 8, taps), lambda g: (0, 0, 0))
    anywhere = pl.BlockSpec(memory_space=pl.ANY)
    full = jax.ShapeDtypeStruct((row_count, width), BF)

    def scratch(count):
        return [
            pltpu.VMEM((filt_count, taps), F32),
            pltpu.VMEM((filt_count, taps), F32),
            pltpu.VMEM((count, taps, 2 * taps), BF),
            pltpu.VMEM((count, taps, 2 * taps), BF),
            pltpu.VMEM((count, taps, 2 * taps), F32),
        ]

    work = 3 * 2 * row_count * 2 * taps * width
    gate_grad, key_grad, value_grad, part = pl.pallas_call(
        functools.partial(inner_kernel, blocks, chan_group),
        grid=(steps,),
        in_specs=[smem, smem, whole, strip, strip, strip, strip],
        out_specs=[strip, strip, strip, table],
        out_shape=[full, full, full, jax.ShapeDtypeStruct((filt_count, 8, taps), F32)],
        scratch_shapes=scratch(blocks - 1),
        compiler_params=pltpu.CompilerParams(vmem_limit_bytes=32 * 2**20),
        cost_estimate=pl.CostEstimate(
            flops=16 * work, bytes_accessed=7 * 2 * row_count * width, transcendentals=0
        ),
        name="inner",
    )(base, lengths, filters, gate, key, value, cotangent)
    gate_grad, key_grad, value_grad, local = pl.pallas_call(
        functools.partial(edge_kernel, blocks, chan_group, scale),
        grid=(steps,),
        in_specs=[smem, smem, whole, top, top, top, top, bottom, bottom, top, top, bottom, bottom]
        + [table, anywhere, anywhere, anywhere],
        out_specs=[top, bottom, bottom, whole],
        out_shape=[full, full, full, jax.ShapeDtypeStruct((taps, filt_count), F32)],
        scratch_shapes=scratch(1) + [pltpu.VMEM((filt_count, 8, taps), F32)],
        input_output_aliases={14: 0, 15: 1, 16: 2},
        compiler_params=pltpu.CompilerParams(vmem_limit_bytes=32 * 2**20),
        cost_estimate=pl.CostEstimate(
            flops=8 * work, bytes_accessed=4 * 2 * row_count * width, transcendentals=0
        ),
        name="edge",
    )(
        base, lengths, filters, prev, later, key, value, key, value,
        gate, cotangent, gate, cotangent, part, gate_grad, key_grad, value_grad,
    )
    filter_grad = lax.psum_scatter(local, "ctx", scatter_dimension=0, tiled=True)
    return (gate_grad, key_grad, value_grad, filter_grad)


def solution(mesh):
    return jax.shard_map(
        on_device,
        mesh=mesh,
        in_specs=(
            P("ctx", "tp"),
            P("ctx", "tp"),
            P("ctx", "tp"),
            P(None, "tp"),
            P(),
            P("ctx", "tp"),
        ),
        out_specs=(P("ctx", "tp"), P("ctx", "tp"), P("ctx", "tp"), P("ctx", "tp")),
        check_vma=False,
    )
```

```python
import functools
import math

import jax
import jax.numpy as jnp
from jax import lax
from jax.experimental import pallas as pl
from jax.experimental.pallas import tpu as pltpu
from jax.sharding import PartitionSpec as P

BF = jnp.bfloat16
F32 = jnp.float32
CHUNK = 128


def doc_ids(lengths_ref, first, shape, dim):
    tokens = first + lax.broadcasted_iota(jnp.int32, shape, dim)

    def add(d, carry):
        end, ids = carry
        end = end + lengths_ref[d]
        return (end, ids + jnp.where(tokens >= end, 1, 0))

    return lax.fori_loop(
        0, lengths_ref.shape[0], add, (jnp.int32(0), jnp.zeros(shape, jnp.int32)), unroll=4
    )[1]


def fill_taps(filters_ref, taps_f, taps_b):
    taps, count = filters_ref.shape
    row = lax.broadcasted_iota(jnp.int32, (taps, taps), 0)
    col = lax.broadcasted_iota(jnp.int32, (taps, taps), 1)
    same = jnp.where(row == col, 1.0, 0.0).astype(BF)
    flip = jnp.where(((row + col) & (taps - 1)) == 0, 1.0, 0.0).astype(BF)
    dims = (((0,), (0,)), ((), ()))
    table = filters_ref[...]
    taps_b[...] = lax.dot_general(table, same, dims, preferred_element_type=F32)
    taps_f[...] = lax.dot_general(table, flip, dims, preferred_element_type=F32)


def band_masks(lengths_ref, first, forward):
    taps = CHUNK
    row = lax.broadcasted_iota(jnp.int32, (taps, taps), 0)
    col = lax.broadcasted_iota(jnp.int32, (taps, taps), 1)
    mine = doc_ids(lengths_ref, first, (taps, taps), 0)
    low = first - taps if forward else first
    near = doc_ids(lengths_ref, low, (8, taps), 1)[:1]
    far = doc_ids(lengths_ref, low + taps, (8, taps), 1)[:1]
    if forward:
        bands = (col > row, col <= row)
    else:
        bands = (col >= row, col < row)
    left = jnp.where((mine == near) & bands[0], 1.0, 0.0)
    right = jnp.where((mine == far) & bands[1], 1.0, 0.0)
    return left, right


def convolve(tap_rows, mask_ref, lhs_ref, inputs, chan_group):
    taps = CHUNK
    lane = lax.broadcasted_iota(jnp.int32, (taps, taps), 1)
    per = tap_rows.shape[0]
    for f in range(per):
        spread = jnp.broadcast_to(tap_rows[f : f + 1], (taps, taps))
        circ = pltpu.roll(spread, 0, 1, stride=1, stride_axis=0).astype(BF)
        for i in range(len(inputs)):
            lhs_ref[i, f * taps : (f + 1) * taps, :taps] = circ * mask_ref[i, :, :taps]
            lhs_ref[i, f * taps : (f + 1) * taps, taps:] = circ * mask_ref[i, :, taps:]
    outs = []
    for i, x in enumerate(inputs):
        got = jnp.dot(lhs_ref[i], x, preferred_element_type=F32)
        total = got[:taps]
        for f in range(1, per):
            total = jnp.where(lane >= f * chan_group, got[f * taps : (f + 1) * taps], total)
        outs.append(total)
    return outs


def correlate(cots, windows, masks, chan_group):
    taps = CHUNK
    lane = lax.broadcasted_iota(jnp.int32, (1, taps), 1)
    per = taps // chan_group
    totals = [None] * per
    picks = [
        jnp.where((lane >= f * chan_group) & (lane < (f + 1) * chan_group), 1.0, 0.0).astype(BF)
        for f in range(per)
    ]
    for cot, window, mask in zip(cots, windows, masks):
        stacked = jnp.concatenate([cot * pick for pick in picks], axis=0)
        every = lax.dot_general(
            stacked, window, (((1,), (1,)), ((), ())), preferred_element_type=F32
        )
        for f in range(per):
            got = every[f * taps : (f + 1) * taps] * mask[...]
            got = got[:, :taps] + got[:, taps:]
            totals[f] = got if totals[f] is None else totals[f] + got
    sums = []
    for total in totals:
        held = total[:8]
        for q in range(1, taps // 8):
            held = held + pltpu.roll(total[8 * q : 8 * q + 8], taps - 8 * q, 1)
        sums.append(held)
    return sums


def collapse(corr_ref, scale):
    taps = CHUNK
    total = corr_ref[:, 0, :]
    for r in range(1, 8):
        total = total + pltpu.roll(corr_ref[:, r, :], taps - r, 1)
    row = lax.broadcasted_iota(jnp.int32, (taps, taps), 0)
    col = lax.broadcasted_iota(jnp.int32, (taps, taps), 1)
    flip = jnp.where(((row + col) & (taps - 1)) == 0, scale, 0.0)
    return lax.dot_general(
        flip, total, (((1,), (1,)), ((), ())),
        precision=lax.Precision.HIGHEST, preferred_element_type=F32,
    )


def exchange_kernel(
    n, blocks, chan_group, scale, lengths_ref, gate_ref, key_ref, value_ref, cot_ref,
    key_tail, value_tail, gate_head, cot_head,
    prev_ref, later_ref, grad_ref,
    send_p, send_c, got_p, got_c, tops, mask_c, corr_ref, local_ref, parts_ref,
    halo_send, halo_recv, part_send, part_recv,
):
    taps = CHUNK
    step = pl.program_id(0)
    steps = pl.num_programs(0) // 2
    per = CHUNK // chan_group
    me = lax.axis_index("ctx")
    share = taps // n

    def halo(source, target, slot, peer):
        return pltpu.make_async_remote_copy(
            src_ref=source,
            dst_ref=target,
            send_sem=halo_send.at[slot],
            recv_sem=halo_recv.at[slot],
            device_id={"ctx": peer},
            device_id_type=pl.DeviceIdType.MESH,
        )

    right, left = lax.rem(me + 1, n), lax.rem(me + n - 1, n)

    @pl.when(step == 0)
    def _():
        barrier = pltpu.get_barrier_semaphore()
        for k in range(1, n):
            pl.semaphore_signal(
                barrier,
                inc=1,
                device_id={"ctx": lax.rem(me + k, n)},
                device_id_type=pl.DeviceIdType.MESH,
            )
        send_p[...] = (key_tail[...].astype(F32) * value_tail[...].astype(F32)).astype(BF)
        send_c[...] = (cot_head[...].astype(F32) * gate_head[...].astype(F32)).astype(BF)
        pl.semaphore_wait(barrier, n - 1)

        @pl.when(me < n - 1)
        def _():
            halo(send_p, got_p, 0, right).start()

        @pl.when(me > 0)
        def _():
            halo(send_c, got_c, 1, left).start()

        @pl.when(me == 0)
        def _():
            got_p[...] = jnp.zeros_like(got_p)

        @pl.when(me == n - 1)
        def _():
            got_c[...] = jnp.zeros_like(got_c)

        for i in range(blocks):
            first = (me * blocks + i) * taps
            mask_c[i, :, :taps], mask_c[i, :, taps:] = band_masks(lengths_ref, first, True)

    @pl.when(step < steps)
    def _():
        product = (key_ref[...].astype(F32) * value_ref[...].astype(F32)).astype(BF)
        filt_cot = (
            cot_ref[taps:].astype(F32) * gate_ref[taps:].astype(F32)
        ).astype(BF)
        tops[step] = product[:taps]
        inner = range(1, blocks)
        cots = [filt_cot[(i - 1) * taps : i * taps] for i in inner]
        windows = [product[(i - 1) * taps : (i + 1) * taps] for i in inner]
        sums = correlate(cots, windows, [mask_c.at[i] for i in inner], chan_group)
        for f in range(per):
            corr_ref[step * per + f] = sums[f]

    @pl.when(step == steps)
    def _():
        @pl.when(me < n - 1)
        def _():
            halo(send_p, got_p, 0, right).wait_send()
            halo(send_c, got_c, 1, right).wait_recv()

        @pl.when(me > 0)
        def _():
            halo(send_c, got_c, 1, left).wait_send()
            halo(send_p, got_p, 0, left).wait_recv()

        prev_ref[...] = got_p[...]
        later_ref[...] = got_c[...]

    @pl.when(step >= steps)
    def _():
        g = step - steps
        lanes = pl.ds(pl.multiple_of(g * CHUNK, CHUNK), CHUNK)
        window = jnp.concatenate([got_p[:, lanes], tops[g]], axis=0)
        sums = correlate([send_c[:, lanes]], [window], [mask_c.at[0]], chan_group)
        for f in range(per):
            corr_ref[g * per + f] = corr_ref[g * per + f] + sums[f]

    @pl.when(step == 2 * steps - 1)
    def _():
        local = collapse(corr_ref, scale)
        for i in range(n):
            local_ref[i] = local[i * share : (i + 1) * share]

        def part(k):
            peer = lax.rem(me + k, n)
            return pltpu.make_async_remote_copy(
                src_ref=local_ref.at[peer],
                dst_ref=parts_ref.at[k],
                send_sem=part_send.at[k],
                recv_sem=part_recv.at[k],
                device_id={"ctx": peer},
                device_id_type=pl.DeviceIdType.MESH,
            )

        for k in range(1, n):
            part(k).start()
        total = local_ref[me]
        for k in range(1, n):
            part(k).wait()
            total = total + parts_ref[k]
        grad_ref[...] = total


def filter_kernel(
    blocks, chan_group, base_ref, lengths_ref, filters_ref, gate_ref, key_ref, value_ref, cot_ref,
    prev_ref, later_ref,
    gg_ref, kg_ref, vg_ref, taps_f, taps_b, mask_f, mask_b, lhs_f, lhs_b,
):
    taps = CHUNK

    @pl.when(pl.program_id(0) == 0)
    def _():
        fill_taps(filters_ref, taps_f, taps_b)
        for i in range(blocks):
            first = base_ref[0] + i * taps
            for mask, forward in ((mask_f, True), (mask_b, False)):
                left, right = band_masks(lengths_ref, first, forward)
                mask[i, :, :taps] = left.astype(BF)
                mask[i, :, taps:] = right.astype(BF)

    per = CHUNK // chan_group
    here = pl.ds(pl.multiple_of(pl.program_id(0) * per, per), per)
    key = key_ref[...].astype(F32)
    value = value_ref[...].astype(F32)
    cot = cot_ref[...].astype(F32)
    product = jnp.concatenate([prev_ref[...], (key * value).astype(BF)], axis=0)
    filt_cot = jnp.concatenate(
        [(cot * gate_ref[...].astype(F32)).astype(BF), later_ref[...]], axis=0
    )
    windows = [product[i * taps : (i + 2) * taps] for i in range(blocks)]
    outs = convolve(taps_f[here], mask_f, lhs_f, windows, chan_group)
    for i, out in enumerate(outs):
        rows = slice(i * taps, (i + 1) * taps)
        gg_ref[rows] = (cot[rows] * out).astype(BF)
    ahead = [filt_cot[i * taps : (i + 2) * taps] for i in range(blocks)]
    outs = convolve(taps_b[here], mask_b, lhs_b, ahead, chan_group)
    for i, out in enumerate(outs):
        rows = slice(i * taps, (i + 1) * taps)
        kg_ref[rows] = (out * value[rows]).astype(BF)
        vg_ref[rows] = (out * key[rows]).astype(BF)


def on_device(gate, key, value, filters, lengths, cotangent):
    row_count, width = gate.shape
    taps, filt_count = filters.shape
    chan_group = width // filt_count
    blocks = row_count // taps
    ctx_count = lax.axis_size("ctx")
    share = taps // ctx_count
    base = (lax.axis_index("ctx") * row_count).astype(jnp.int32).reshape(1)
    scale = 1.0 / math.sqrt(row_count * ctx_count)
    steps = width // CHUNK
    per = CHUNK // chan_group
    smem = pl.BlockSpec(memory_space=pltpu.SMEM)
    strip = pl.BlockSpec((row_count, CHUNK), lambda g: (0, g))
    once = pl.BlockSpec((row_count, CHUNK), lambda g: (0, jnp.minimum(g, steps - 1)))
    head = pl.BlockSpec((taps, width), lambda g: (0, 0))
    bottom = pl.BlockSpec((taps, width), lambda g: (blocks - 1, 0))
    top = pl.BlockSpec((taps, CHUNK), lambda g: (0, g))
    full = jax.ShapeDtypeStruct((row_count, width), BF)
    edge = jax.ShapeDtypeStruct((taps, width), BF)
    wide = pltpu.VMEM((taps, width), BF)
    prev, later, filter_grad = pl.pallas_call(
        functools.partial(exchange_kernel, ctx_count, blocks, chan_group, scale),
        grid=(2 * steps,),
        in_specs=[smem, once, once, once, once, bottom, bottom, head, head],
        out_specs=[head, head, pl.BlockSpec((share, filt_count), lambda g: (0, 0))],
        out_shape=[edge, edge, jax.ShapeDtypeStruct((share, filt_count), F32)],
        scratch_shapes=[
            wide, wide, wide, wide,
            pltpu.VMEM((steps, taps, CHUNK), BF),
            pltpu.VMEM((blocks, taps, 2 * taps), F32),
            pltpu.VMEM((filt_count, 8, taps), F32),
            pltpu.VMEM((ctx_count, share, filt_count), F32),
            pltpu.VMEM((ctx_count, share, filt_count), F32),
            pltpu.SemaphoreType.DMA((2,)),
            pltpu.SemaphoreType.DMA((2,)),
            pltpu.SemaphoreType.DMA((ctx_count,)),
            pltpu.SemaphoreType.DMA((ctx_count,)),
        ],
        compiler_params=pltpu.CompilerParams(
            vmem_limit_bytes=40 * 2**20, collective_id=0, has_side_effects=True
        ),
        name="exchange",
    )(lengths, gate, key, value, cotangent, key, value, gate, cotangent)
    gate_grad, key_grad, value_grad = pl.pallas_call(
        functools.partial(filter_kernel, blocks, chan_group),
        grid=(steps,),
        in_specs=[
            smem, smem, pl.BlockSpec((taps, filt_count), lambda g: (0, 0)),
            strip, strip, strip, strip, top, top,
        ],
        out_specs=[strip, strip, strip],
        out_shape=[full, full, full],
        scratch_shapes=[
            pltpu.VMEM((filt_count, taps), F32),
            pltpu.VMEM((filt_count, taps), F32),
            pltpu.VMEM((blocks, taps, 2 * taps), BF),
            pltpu.VMEM((blocks, taps, 2 * taps), BF),
            pltpu.VMEM((blocks, per * taps, 2 * taps), BF),
            pltpu.VMEM((blocks, per * taps, 2 * taps), BF),
        ],
        compiler_params=pltpu.CompilerParams(vmem_limit_bytes=40 * 2**20),
        name="filter",
    )(base, lengths, filters, gate, key, value, cotangent, prev, later)
    return (gate_grad, key_grad, value_grad, filter_grad)


def solution(mesh):
    return jax.shard_map(
        on_device,
        mesh=mesh,
        in_specs=(
            P("ctx", "tp"),
            P("ctx", "tp"),
            P("ctx", "tp"),
            P(None, "tp"),
            P(),
            P("ctx", "tp"),
        ),
        out_specs=(P("ctx", "tp"), P("ctx", "tp"), P("ctx", "tp"), P("ctx", "tp")),
        check_vma=False,
    )
```

```python
import functools
import math

import jax
import jax.numpy as jnp
from jax import lax
from jax.experimental import pallas as pl
from jax.experimental.pallas import tpu as pltpu
from jax.sharding import PartitionSpec as P

BF = jnp.bfloat16
F32 = jnp.float32
CHUNK = 128
PAIR = 2
GRANT = 62 * 2**20


def doc_ids(lengths_ref, first, shape, dim):
    tokens = first + lax.broadcasted_iota(jnp.int32, shape, dim)

    def add(d, carry):
        end, ids = carry
        end = end + lengths_ref[d]
        return (end, ids + jnp.where(tokens >= end, 1, 0))

    return lax.fori_loop(
        0, lengths_ref.shape[0], add, (jnp.int32(0), jnp.zeros(shape, jnp.int32)), unroll=4
    )[1]


def fill_taps(filters_ref, taps_f, taps_b):
    taps, count = filters_ref.shape
    row = lax.broadcasted_iota(jnp.int32, (taps, taps), 0)
    col = lax.broadcasted_iota(jnp.int32, (taps, taps), 1)
    same = jnp.where(row == col, 1.0, 0.0).astype(BF)
    flip = jnp.where(((row + col) & (taps - 1)) == 0, 1.0, 0.0).astype(BF)
    dims = (((0,), (0,)), ((), ()))
    table = filters_ref[...]
    taps_b[...] = lax.dot_general(table, same, dims, preferred_element_type=F32)
    taps_f[...] = lax.dot_general(table, flip, dims, preferred_element_type=F32)


def band_masks(lengths_ref, first, forward):
    taps = CHUNK
    row = lax.broadcasted_iota(jnp.int32, (taps, taps), 0)
    col = lax.broadcasted_iota(jnp.int32, (taps, taps), 1)
    mine = doc_ids(lengths_ref, first, (taps, taps), 0)
    low = first - taps if forward else first
    near = doc_ids(lengths_ref, low, (8, taps), 1)[:1]
    far = doc_ids(lengths_ref, low + taps, (8, taps), 1)[:1]
    if forward:
        bands = (col > row, col <= row)
    else:
        bands = (col >= row, col < row)
    left = jnp.where((mine == near) & bands[0], 1.0, 0.0)
    right = jnp.where((mine == far) & bands[1], 1.0, 0.0)
    return left, right


def convolve(tap_rows, mask_ref, lhs_ref, inputs, chan_group):
    taps = CHUNK
    lane = lax.broadcasted_iota(jnp.int32, (taps, taps), 1)
    per = tap_rows.shape[0]
    for f in range(per):
        spread = jnp.broadcast_to(tap_rows[f : f + 1], (taps, taps))
        circ = pltpu.roll(spread, 0, 1, stride=1, stride_axis=0).astype(BF)
        for i in range(len(inputs)):
            lhs_ref[i, f * taps : (f + 1) * taps, :taps] = circ * mask_ref[i, :, :taps]
            lhs_ref[i, f * taps : (f + 1) * taps, taps:] = circ * mask_ref[i, :, taps:]
    outs = []
    for i, x in enumerate(inputs):
        got = jnp.dot(lhs_ref[i], x, preferred_element_type=F32)
        total = got[:taps]
        for f in range(1, per):
            total = jnp.where(lane >= f * chan_group, got[f * taps : (f + 1) * taps], total)
        outs.append(total)
    return outs


def correlate(cots, windows, masks, chan_group):
    taps = CHUNK
    lane = lax.broadcasted_iota(jnp.int32, (1, taps), 1)
    before = lax.broadcasted_iota(jnp.int32, (taps, taps), 1) > lax.broadcasted_iota(
        jnp.int32, (taps, taps), 0
    )
    per = taps // chan_group
    totals = [None] * per
    picks = [
        jnp.where((lane >= f * chan_group) & (lane < (f + 1) * chan_group), 1.0, 0.0).astype(BF)
        for f in range(per)
    ]
    for cot, window, mask in zip(cots, windows, masks):
        stacked = jnp.concatenate([cot * pick for pick in picks], axis=0)
        every = lax.dot_general(
            stacked, window, (((1,), (1,)), ((), ())), preferred_element_type=F32
        )
        for f in range(per):
            got = every[f * taps : (f + 1) * taps]
            got = jnp.where(before, got[:, :taps], got[:, taps:]) * mask[...]
            totals[f] = got if totals[f] is None else totals[f] + got
    sums = []
    for total in totals:
        held = total[:8]
        for q in range(1, taps // 8):
            held = held + pltpu.roll(total[8 * q : 8 * q + 8], taps - 8 * q, 1)
        sums.append(held)
    return sums


def collapse(corr_ref, scale):
    taps = CHUNK
    total = corr_ref[:, 0, :]
    for r in range(1, 8):
        total = total + pltpu.roll(corr_ref[:, r, :], taps - r, 1)
    row = lax.broadcasted_iota(jnp.int32, (taps, taps), 0)
    col = lax.broadcasted_iota(jnp.int32, (taps, taps), 1)
    flip = jnp.where(((row + col) & (taps - 1)) == 0, scale, 0.0)
    return lax.dot_general(
        flip, total, (((1,), (1,)), ((), ())),
        precision=lax.Precision.HIGHEST, preferred_element_type=F32,
    )


def exchange_kernel(
    n, blocks, chan_group, scale, lengths_ref, gate_ref, key_ref, value_ref, cot_ref,
    key_tail, value_tail, gate_head, cot_head,
    prev_ref, later_ref, grad_ref,
    send_p, send_c, got_p, got_c, tops, mask_c, corr_ref, local_ref, parts_ref,
    halo_send, halo_recv, part_send, part_recv,
):
    taps = CHUNK
    step = pl.program_id(0)
    steps = pl.num_programs(0) - 1
    per = CHUNK // chan_group
    me = lax.axis_index("ctx")
    share = taps // n

    def halo(source, target, slot, peer):
        return pltpu.make_async_remote_copy(
            src_ref=source,
            dst_ref=target,
            send_sem=halo_send.at[slot],
            recv_sem=halo_recv.at[slot],
            device_id={"ctx": peer},
            device_id_type=pl.DeviceIdType.MESH,
        )

    right, left = lax.rem(me + 1, n), lax.rem(me + n - 1, n)

    @pl.when(step == 0)
    def _():
        barrier = pltpu.get_barrier_semaphore()
        for k in range(1, n):
            pl.semaphore_signal(
                barrier,
                inc=1,
                device_id={"ctx": lax.rem(me + k, n)},
                device_id_type=pl.DeviceIdType.MESH,
            )
        send_p[...] = (key_tail[...].astype(F32) * value_tail[...].astype(F32)).astype(BF)
        send_c[...] = (cot_head[...].astype(F32) * gate_head[...].astype(F32)).astype(BF)
        pl.semaphore_wait(barrier, n - 1)

        @pl.when(me < n - 1)
        def _():
            halo(send_p, got_p, 0, right).start()

        @pl.when(me > 0)
        def _():
            halo(send_c, got_c, 1, left).start()

        @pl.when(me == 0)
        def _():
            got_p[...] = jnp.zeros_like(got_p)

        @pl.when(me == n - 1)
        def _():
            got_c[...] = jnp.zeros_like(got_c)

        for i in range(blocks):
            first = (me * blocks + i) * taps
            lower, upper = band_masks(lengths_ref, first, True)
            mask_c[i] = lower + upper

    @pl.when(step < steps)
    def _():
        product = (key_ref[...].astype(F32) * value_ref[...].astype(F32)).astype(BF)
        filt_cot = (
            cot_ref[taps:].astype(F32) * gate_ref[taps:].astype(F32)
        ).astype(BF)
        inner = range(1, blocks)
        for p in range(PAIR):
            lanes = slice(p * CHUNK, (p + 1) * CHUNK)
            g = step * PAIR + p
            tops[g] = product[:taps, lanes]
            cots = [filt_cot[(i - 1) * taps : i * taps, lanes] for i in inner]
            windows = [product[(i - 1) * taps : (i + 1) * taps, lanes] for i in inner]
            sums = correlate(cots, windows, [mask_c.at[i] for i in inner], chan_group)
            for f in range(per):
                corr_ref[g * per + f] = sums[f]

    @pl.when(step == steps)
    def _():
        @pl.when(me < n - 1)
        def _():
            halo(send_p, got_p, 0, right).wait_send()
            halo(send_c, got_c, 1, right).wait_recv()

        @pl.when(me > 0)
        def _():
            halo(send_c, got_c, 1, left).wait_send()
            halo(send_p, got_p, 0, left).wait_recv()

        prev_ref[...] = got_p[...]
        later_ref[...] = got_c[...]

        def edge(g, carry):
            lanes = pl.ds(pl.multiple_of(g * CHUNK, CHUNK), CHUNK)
            window = jnp.concatenate([got_p[:, lanes], tops[g]], axis=0)
            sums = correlate([send_c[:, lanes]], [window], [mask_c.at[0]], chan_group)
            for f in range(per):
                corr_ref[g * per + f] = corr_ref[g * per + f] + sums[f]
            return carry

        lax.fori_loop(0, steps * PAIR, edge, 0, unroll=2)
        local = collapse(corr_ref, scale)
        for i in range(n):
            local_ref[i] = local[i * share : (i + 1) * share]

        def part(k):
            peer = lax.rem(me + k, n)
            return pltpu.make_async_remote_copy(
                src_ref=local_ref.at[peer],
                dst_ref=parts_ref.at[k],
                send_sem=part_send.at[k],
                recv_sem=part_recv.at[k],
                device_id={"ctx": peer},
                device_id_type=pl.DeviceIdType.MESH,
            )

        for k in range(1, n):
            part(k).start()
        total = local_ref[me]
        for k in range(1, n):
            part(k).wait()
            total = total + parts_ref[k]
        grad_ref[...] = total


def filter_kernel(
    blocks, chan_group, base_ref, lengths_ref, filters_ref, gate_ref, key_ref, value_ref, cot_ref,
    prev_ref, later_ref,
    gg_ref, kg_ref, vg_ref, taps_f, taps_b, mask_f, mask_b, lhs_f, lhs_b,
):
    taps = CHUNK

    @pl.when(pl.program_id(0) == 0)
    def _():
        fill_taps(filters_ref, taps_f, taps_b)
        for i in range(blocks):
            first = base_ref[0] + i * taps
            for mask, forward in ((mask_f, True), (mask_b, False)):
                left, right = band_masks(lengths_ref, first, forward)
                mask[i, :, :taps] = left.astype(BF)
                mask[i, :, taps:] = right.astype(BF)

    per = CHUNK // chan_group
    for p in range(PAIR):
        lanes = slice(p * CHUNK, (p + 1) * CHUNK)
        here = pl.ds(pl.multiple_of((pl.program_id(0) * PAIR + p) * per, per), per)
        key = key_ref[:, lanes].astype(F32)
        value = value_ref[:, lanes].astype(F32)
        cot = cot_ref[:, lanes].astype(F32)
        product = jnp.concatenate([prev_ref[:, lanes], (key * value).astype(BF)], axis=0)
        filt_cot = jnp.concatenate(
            [(cot * gate_ref[:, lanes].astype(F32)).astype(BF), later_ref[:, lanes]], axis=0
        )
        windows = [product[i * taps : (i + 2) * taps] for i in range(blocks)]
        outs = convolve(taps_f[here], mask_f, lhs_f.at[p], windows, chan_group)
        for i, out in enumerate(outs):
            rows = slice(i * taps, (i + 1) * taps)
            gg_ref[rows, lanes] = (cot[rows] * out).astype(BF)
        ahead = [filt_cot[i * taps : (i + 2) * taps] for i in range(blocks)]
        outs = convolve(taps_b[here], mask_b, lhs_b.at[p], ahead, chan_group)
        for i, out in enumerate(outs):
            rows = slice(i * taps, (i + 1) * taps)
            kg_ref[rows, lanes] = (out * value[rows]).astype(BF)
            vg_ref[rows, lanes] = (out * key[rows]).astype(BF)


def on_device(gate, key, value, filters, lengths, cotangent):
    row_count, width = gate.shape
    taps, filt_count = filters.shape
    chan_group = width // filt_count
    blocks = row_count // taps
    ctx_count = lax.axis_size("ctx")
    share = taps // ctx_count
    base = (lax.axis_index("ctx") * row_count).astype(jnp.int32).reshape(1)
    scale = 1.0 / math.sqrt(row_count * ctx_count)
    steps = width // (PAIR * CHUNK)
    per = CHUNK // chan_group
    smem = pl.BlockSpec(memory_space=pltpu.SMEM)
    strip = pl.BlockSpec((row_count, PAIR * CHUNK), lambda g: (0, g))
    once = pl.BlockSpec((row_count, PAIR * CHUNK), lambda g: (0, jnp.minimum(g, steps - 1)))
    head = pl.BlockSpec((taps, width), lambda g: (0, 0))
    bottom = pl.BlockSpec((taps, width), lambda g: (blocks - 1, 0))
    top = pl.BlockSpec((taps, PAIR * CHUNK), lambda g: (0, g))
    full = jax.ShapeDtypeStruct((row_count, width), BF)
    edge = jax.ShapeDtypeStruct((taps, width), BF)
    wide = pltpu.VMEM((taps, width), BF)
    prev, later, filter_grad = pl.pallas_call(
        functools.partial(exchange_kernel, ctx_count, blocks, chan_group, scale),
        grid=(steps + 1,),
        in_specs=[smem, once, once, once, once, bottom, bottom, head, head],
        out_specs=[head, head, pl.BlockSpec((share, filt_count), lambda g: (0, 0))],
        out_shape=[edge, edge, jax.ShapeDtypeStruct((share, filt_count), F32)],
        scratch_shapes=[
            wide, wide, wide, wide,
            pltpu.VMEM((steps * PAIR, taps, CHUNK), BF),
            pltpu.VMEM((blocks, taps, taps), F32),
            pltpu.VMEM((filt_count, 8, taps), F32),
            pltpu.VMEM((ctx_count, share, filt_count), F32),
            pltpu.VMEM((ctx_count, share, filt_count), F32),
            pltpu.SemaphoreType.DMA((2,)),
            pltpu.SemaphoreType.DMA((2,)),
            pltpu.SemaphoreType.DMA((ctx_count,)),
            pltpu.SemaphoreType.DMA((ctx_count,)),
        ],
        compiler_params=pltpu.CompilerParams(
            vmem_limit_bytes=GRANT, collective_id=0, has_side_effects=True
        ),
        name="exchange",
    )(lengths, gate, key, value, cotangent, key, value, gate, cotangent)
    gate_grad, key_grad, value_grad = pl.pallas_call(
        functools.partial(filter_kernel, blocks, chan_group),
        grid=(steps,),
        in_specs=[
            smem, smem, pl.BlockSpec((taps, filt_count), lambda g: (0, 0)),
            strip, strip, strip, strip, top, top,
        ],
        out_specs=[strip, strip, strip],
        out_shape=[full, full, full],
        scratch_shapes=[
            pltpu.VMEM((filt_count, taps), F32),
            pltpu.VMEM((filt_count, taps), F32),
            pltpu.VMEM((blocks, taps, 2 * taps), BF),
            pltpu.VMEM((blocks, taps, 2 * taps), BF),
            pltpu.VMEM((PAIR, blocks, per * taps, 2 * taps), BF),
            pltpu.VMEM((PAIR, blocks, per * taps, 2 * taps), BF),
        ],
        compiler_params=pltpu.CompilerParams(vmem_limit_bytes=GRANT),
        name="filter",
    )(base, lengths, filters, gate, key, value, cotangent, prev, later)
    return (gate_grad, key_grad, value_grad, filter_grad)


def solution(mesh):
    return jax.shard_map(
        on_device,
        mesh=mesh,
        in_specs=(
            P("ctx", "tp"),
            P("ctx", "tp"),
            P("ctx", "tp"),
            P(None, "tp"),
            P(),
            P("ctx", "tp"),
        ),
        out_specs=(P("ctx", "tp"), P("ctx", "tp"), P("ctx", "tp"), P("ctx", "tp")),
        check_vma=False,
    )
```

```python
import functools
import math

import jax
import jax.numpy as jnp
from jax import lax
from jax.experimental import pallas as pl
from jax.experimental.pallas import tpu as pltpu
from jax.sharding import PartitionSpec as P

BF = jnp.bfloat16
F32 = jnp.float32
CHUNK = 128
PAIR = 2
GRANT = 62 * 2**20


def doc_ids(lengths_ref, first, shape, dim):
    tokens = first + lax.broadcasted_iota(jnp.int32, shape, dim)

    def add(d, carry):
        end, ids = carry
        end = end + lengths_ref[d]
        return (end, ids + jnp.where(tokens >= end, 1, 0))

    return lax.fori_loop(
        0, lengths_ref.shape[0], add, (jnp.int32(0), jnp.zeros(shape, jnp.int32)), unroll=4
    )[1]


def fill_taps(filters_ref, taps_f, taps_b):
    taps, count = filters_ref.shape
    row = lax.broadcasted_iota(jnp.int32, (taps, taps), 0)
    col = lax.broadcasted_iota(jnp.int32, (taps, taps), 1)
    same = jnp.where(row == col, 1.0, 0.0).astype(BF)
    flip = jnp.where(((row + col) & (taps - 1)) == 0, 1.0, 0.0).astype(BF)
    dims = (((0,), (0,)), ((), ()))
    table = filters_ref[...]
    taps_b[...] = lax.dot_general(table, same, dims, preferred_element_type=F32)
    taps_f[...] = lax.dot_general(table, flip, dims, preferred_element_type=F32)


def band_masks(lengths_ref, first, forward):
    taps = CHUNK
    row = lax.broadcasted_iota(jnp.int32, (taps, taps), 0)
    col = lax.broadcasted_iota(jnp.int32, (taps, taps), 1)
    mine = doc_ids(lengths_ref, first, (taps, taps), 0)
    low = first - taps if forward else first
    near = doc_ids(lengths_ref, low, (8, taps), 1)[:1]
    far = doc_ids(lengths_ref, low + taps, (8, taps), 1)[:1]
    if forward:
        bands = (col > row, col <= row)
    else:
        bands = (col >= row, col < row)
    left = jnp.where((mine == near) & bands[0], 1.0, 0.0)
    right = jnp.where((mine == far) & bands[1], 1.0, 0.0)
    return left, right


def convolve(tap_rows, mask_ref, inputs, chan_group):
    taps = CHUNK
    lane = lax.broadcasted_iota(jnp.int32, (taps, taps), 1)
    per = tap_rows.shape[0]
    outs = [None] * len(inputs)
    for f in range(per):
        spread = jnp.broadcast_to(tap_rows[f : f + 1], (taps, taps))
        circ = pltpu.roll(spread, 0, 1, stride=1, stride_axis=0).astype(BF)
        for i, x in enumerate(inputs):
            banded = jnp.concatenate(
                [circ * mask_ref[i, :, :taps], circ * mask_ref[i, :, taps:]], axis=1
            )
            got = jnp.dot(banded, x, preferred_element_type=F32)
            outs[i] = got if f == 0 else jnp.where(lane >= f * chan_group, got, outs[i])
    return outs


def correlate(cots, windows, masks, chan_group):
    taps = CHUNK
    lane = lax.broadcasted_iota(jnp.int32, (1, taps), 1)
    before = lax.broadcasted_iota(jnp.int32, (taps, taps), 1) > lax.broadcasted_iota(
        jnp.int32, (taps, taps), 0
    )
    per = taps // chan_group
    totals = [None] * per
    picks = [
        jnp.where((lane >= f * chan_group) & (lane < (f + 1) * chan_group), 1.0, 0.0).astype(BF)
        for f in range(per)
    ]
    for f in range(per):
        for cot, window, mask in zip(cots, windows, masks):
            got = lax.dot_general(
                cot * picks[f], window, (((1,), (1,)), ((), ())), preferred_element_type=F32
            )
            got = jnp.where(before, got[:, :taps], got[:, taps:]) * mask[...]
            totals[f] = got if totals[f] is None else totals[f] + got
    sums = []
    for total in totals:
        held = total[:8]
        for q in range(1, taps // 8):
            held = held + pltpu.roll(total[8 * q : 8 * q + 8], taps - 8 * q, 1)
        sums.append(held)
    return sums


def collapse(corr_ref, scale):
    taps = CHUNK
    total = corr_ref[:, 0, :]
    for r in range(1, 8):
        total = total + pltpu.roll(corr_ref[:, r, :], taps - r, 1)
    row = lax.broadcasted_iota(jnp.int32, (taps, taps), 0)
    col = lax.broadcasted_iota(jnp.int32, (taps, taps), 1)
    flip = jnp.where(((row + col) & (taps - 1)) == 0, scale, 0.0)
    return lax.dot_general(
        flip, total, (((1,), (1,)), ((), ())),
        precision=lax.Precision.HIGHEST, preferred_element_type=F32,
    )


def exchange_kernel(
    n, blocks, chan_group, scale, lengths_ref, gate_ref, key_ref, value_ref, cot_ref,
    key_tail, value_tail, gate_head, cot_head,
    prev_ref, later_ref, grad_ref,
    send_p, send_c, got_p, got_c, tops, mask_c, corr_ref, local_ref, parts_ref,
    halo_send, halo_recv, part_send, part_recv,
):
    taps = CHUNK
    step = pl.program_id(0)
    steps = pl.num_programs(0) - 1
    per = CHUNK // chan_group
    me = lax.axis_index("ctx")
    share = taps // n

    def halo(source, target, slot, peer):
        return pltpu.make_async_remote_copy(
            src_ref=source,
            dst_ref=target,
            send_sem=halo_send.at[slot],
            recv_sem=halo_recv.at[slot],
            device_id={"ctx": peer},
            device_id_type=pl.DeviceIdType.MESH,
        )

    right, left = lax.rem(me + 1, n), lax.rem(me + n - 1, n)

    @pl.when(step == 0)
    def _():
        barrier = pltpu.get_barrier_semaphore()
        for k in range(1, n):
            pl.semaphore_signal(
                barrier,
                inc=1,
                device_id={"ctx": lax.rem(me + k, n)},
                device_id_type=pl.DeviceIdType.MESH,
            )
        send_p[...] = (key_tail[...].astype(F32) * value_tail[...].astype(F32)).astype(BF)
        send_c[...] = (cot_head[...].astype(F32) * gate_head[...].astype(F32)).astype(BF)
        pl.semaphore_wait(barrier, n - 1)

        @pl.when(me < n - 1)
        def _():
            halo(send_p, got_p, 0, right).start()

        @pl.when(me > 0)
        def _():
            halo(send_c, got_c, 1, left).start()

        @pl.when(me == 0)
        def _():
            got_p[...] = jnp.zeros_like(got_p)

        @pl.when(me == n - 1)
        def _():
            got_c[...] = jnp.zeros_like(got_c)

        for i in range(blocks):
            first = (me * blocks + i) * taps
            lower, upper = band_masks(lengths_ref, first, True)
            mask_c[i] = lower + upper

    @pl.when(step < steps)
    def _():
        product = (key_ref[...].astype(F32) * value_ref[...].astype(F32)).astype(BF)
        filt_cot = (
            cot_ref[taps:].astype(F32) * gate_ref[taps:].astype(F32)
        ).astype(BF)
        inner = range(1, blocks)
        for p in range(PAIR):
            lanes = slice(p * CHUNK, (p + 1) * CHUNK)
            g = step * PAIR + p
            tops[g] = product[:taps, lanes]
            cots = [filt_cot[(i - 1) * taps : i * taps, lanes] for i in inner]
            windows = [product[(i - 1) * taps : (i + 1) * taps, lanes] for i in inner]
            sums = correlate(cots, windows, [mask_c.at[i] for i in inner], chan_group)
            for f in range(per):
                corr_ref[g * per + f] = sums[f]

    @pl.when(step == steps)
    def _():
        @pl.when(me < n - 1)
        def _():
            halo(send_p, got_p, 0, right).wait_send()
            halo(send_c, got_c, 1, right).wait_recv()

        @pl.when(me > 0)
        def _():
            halo(send_c, got_c, 1, left).wait_send()
            halo(send_p, got_p, 0, left).wait_recv()

        prev_ref[...] = got_p[...]
        later_ref[...] = got_c[...]

        def edge(g, carry):
            lanes = pl.ds(pl.multiple_of(g * CHUNK, CHUNK), CHUNK)
            window = jnp.concatenate([got_p[:, lanes], tops[g]], axis=0)
            sums = correlate([send_c[:, lanes]], [window], [mask_c.at[0]], chan_group)
            for f in range(per):
                corr_ref[g * per + f] = corr_ref[g * per + f] + sums[f]
            return carry

        lax.fori_loop(0, steps * PAIR, edge, 0, unroll=2)
        local = collapse(corr_ref, scale)
        for i in range(n):
            local_ref[i] = local[i * share : (i + 1) * share]

        def part(k):
            peer = lax.rem(me + k, n)
            return pltpu.make_async_remote_copy(
                src_ref=local_ref.at[peer],
                dst_ref=parts_ref.at[k],
                send_sem=part_send.at[k],
                recv_sem=part_recv.at[k],
                device_id={"ctx": peer},
                device_id_type=pl.DeviceIdType.MESH,
            )

        for k in range(1, n):
            part(k).start()
        total = local_ref[me]
        for k in range(1, n):
            part(k).wait()
            total = total + parts_ref[k]
        grad_ref[...] = total


def filter_kernel(
    blocks, chan_group, base_ref, lengths_ref, filters_ref, gate_ref, key_ref, value_ref, cot_ref,
    prev_ref, later_ref,
    gg_ref, kg_ref, vg_ref, taps_f, taps_b, mask_f, mask_b,
):
    taps = CHUNK

    @pl.when(pl.program_id(0) == 0)
    def _():
        fill_taps(filters_ref, taps_f, taps_b)
        for i in range(blocks):
            first = base_ref[0] + i * taps
            for mask, forward in ((mask_f, True), (mask_b, False)):
                left, right = band_masks(lengths_ref, first, forward)
                mask[i, :, :taps] = left.astype(BF)
                mask[i, :, taps:] = right.astype(BF)

    per = CHUNK // chan_group
    for p in range(PAIR):
        lanes = slice(p * CHUNK, (p + 1) * CHUNK)
        here = pl.ds(pl.multiple_of((pl.program_id(0) * PAIR + p) * per, per), per)
        key = key_ref[:, lanes].astype(F32)
        value = value_ref[:, lanes].astype(F32)
        cot = cot_ref[:, lanes].astype(F32)
        product = jnp.concatenate([prev_ref[:, lanes], (key * value).astype(BF)], axis=0)
        filt_cot = jnp.concatenate(
            [(cot * gate_ref[:, lanes].astype(F32)).astype(BF), later_ref[:, lanes]], axis=0
        )
        windows = [product[i * taps : (i + 2) * taps] for i in range(blocks)]
        outs = convolve(taps_f[here], mask_f, windows, chan_group)
        for i, out in enumerate(outs):
            rows = slice(i * taps, (i + 1) * taps)
            gg_ref[rows, lanes] = (cot[rows] * out).astype(BF)
        ahead = [filt_cot[i * taps : (i + 2) * taps] for i in range(blocks)]
        outs = convolve(taps_b[here], mask_b, ahead, chan_group)
        for i, out in enumerate(outs):
            rows = slice(i * taps, (i + 1) * taps)
            kg_ref[rows, lanes] = (out * value[rows]).astype(BF)
            vg_ref[rows, lanes] = (out * key[rows]).astype(BF)


def on_device(gate, key, value, filters, lengths, cotangent):
    row_count, width = gate.shape
    taps, filt_count = filters.shape
    chan_group = width // filt_count
    blocks = row_count // taps
    ctx_count = lax.axis_size("ctx")
    share = taps // ctx_count
    base = (lax.axis_index("ctx") * row_count).astype(jnp.int32).reshape(1)
    scale = 1.0 / math.sqrt(row_count * ctx_count)
    steps = width // (PAIR * CHUNK)
    smem = pl.BlockSpec(memory_space=pltpu.SMEM)
    strip = pl.BlockSpec((row_count, PAIR * CHUNK), lambda g: (0, g))
    once = pl.BlockSpec((row_count, PAIR * CHUNK), lambda g: (0, jnp.minimum(g, steps - 1)))
    head = pl.BlockSpec((taps, width), lambda g: (0, 0))
    bottom = pl.BlockSpec((taps, width), lambda g: (blocks - 1, 0))
    top = pl.BlockSpec((taps, PAIR * CHUNK), lambda g: (0, g))
    full = jax.ShapeDtypeStruct((row_count, width), BF)
    edge = jax.ShapeDtypeStruct((taps, width), BF)
    wide = pltpu.VMEM((taps, width), BF)
    prev, later, filter_grad = pl.pallas_call(
        functools.partial(exchange_kernel, ctx_count, blocks, chan_group, scale),
        grid=(steps + 1,),
        in_specs=[smem, once, once, once, once, bottom, bottom, head, head],
        out_specs=[head, head, pl.BlockSpec((share, filt_count), lambda g: (0, 0))],
        out_shape=[edge, edge, jax.ShapeDtypeStruct((share, filt_count), F32)],
        scratch_shapes=[
            wide, wide, wide, wide,
            pltpu.VMEM((steps * PAIR, taps, CHUNK), BF),
            pltpu.VMEM((blocks, taps, taps), F32),
            pltpu.VMEM((filt_count, 8, taps), F32),
            pltpu.VMEM((ctx_count, share, filt_count), F32),
            pltpu.VMEM((ctx_count, share, filt_count), F32),
            pltpu.SemaphoreType.DMA((2,)),
            pltpu.SemaphoreType.DMA((2,)),
            pltpu.SemaphoreType.DMA((ctx_count,)),
            pltpu.SemaphoreType.DMA((ctx_count,)),
        ],
        compiler_params=pltpu.CompilerParams(
            vmem_limit_bytes=GRANT, collective_id=0, has_side_effects=True
        ),
        name="exchange",
    )(lengths, gate, key, value, cotangent, key, value, gate, cotangent)
    gate_grad, key_grad, value_grad = pl.pallas_call(
        functools.partial(filter_kernel, blocks, chan_group),
        grid=(steps,),
        in_specs=[
            smem, smem, pl.BlockSpec((taps, filt_count), lambda g: (0, 0)),
            strip, strip, strip, strip, top, top,
        ],
        out_specs=[strip, strip, strip],
        out_shape=[full, full, full],
        scratch_shapes=[
            pltpu.VMEM((filt_count, taps), F32),
            pltpu.VMEM((filt_count, taps), F32),
            pltpu.VMEM((blocks, taps, 2 * taps), BF),
            pltpu.VMEM((blocks, taps, 2 * taps), BF),
        ],
        compiler_params=pltpu.CompilerParams(vmem_limit_bytes=GRANT),
        name="filter",
    )(base, lengths, filters, gate, key, value, cotangent, prev, later)
    return (gate_grad, key_grad, value_grad, filter_grad)


def solution(mesh):
    return jax.shard_map(
        on_device,
        mesh=mesh,
        in_specs=(
            P("ctx", "tp"),
            P("ctx", "tp"),
            P("ctx", "tp"),
            P(None, "tp"),
            P(),
            P("ctx", "tp"),
        ),
        out_specs=(P("ctx", "tp"), P("ctx", "tp"), P("ctx", "tp"), P("ctx", "tp")),
        check_vma=False,
    )
```
